32 devices in a mesh: groups: 1, dp: 32 (over z, y, x, core).
Axes of the slice: x: 2, y: 2, z: 4, core: 2. Of those that a mesh axis runs over, the one named last changes fastest.
Arguments:
- input_after_norm: bfloat16 [8192, 5120], P(('groups', 'dp')), may hold values from -6 to 6
- value_cotangent: bfloat16 [8192, 1024], P(('groups', 'dp')), may hold values from -6 to 6
- value_weight: bfloat16 [5120, 1024], P('dp'), may hold values from -0.078125 to 0.078125
- down_factors: bfloat16 [5120, 512], P('dp'), may hold values from -0.078125 to 0.078125
- up_factors: bfloat16 [512, 1024], P('dp'), may hold values from -0.1875 to 0.1875
- sequence_adapter: int32 [32], P(('groups', 'dp')), may hold values from 0 to 31
- sequence_loss_length: int32 [32], P(('groups', 'dp')), may hold values from 64 to 256
- adapter_owner_slot: int32 [32], replicated, may hold values from 0 to 31, each once
Outputs:
- input_gradient: bfloat16 [8192, 5120], P(('groups', 'dp'))
- grad_a: float32 [5120, 512], P(('groups', 'dp'))
- grad_b: float32 [512, 1024], P(('groups', 'dp'))
The draws below stay inside these ranges and needn't reach their ends.
Inputs may be any that keep to these rules, and one draw needn't show every extreme that they name: `sequence_adapter`: every id names an adapter. `adapter_owner_slot`: each adapter has its own slot.
All inputs are finite; a program needn't handle non-finite values.
Results may differ from the reference program's by a relative error of at most 0.0031.
Values may be sent and summed in bfloat16 or wider, within the bound.
No kernel may reach another device: no remote copies, remote signals or barrier semaphores. Data moves between devices by JAX's collectives and lax.ppermute only.
A program may use at most 128 MiB of HBM per device.

```python
import math
import jax
import jax.numpy as jnp
import numpy as np
from jax import lax

MODEL_WIDTH = 5120
VALUE_WIDTH = 1024
ADAPTER_RANK = 16
LENGTH = 256
ADAPTER_COUNT = 32
SEQS = 32
TOKENS = 8192


def with_ends(array, own_key, low, high):
    dims = array.shape
    place = [jax.random.randint(jax.random.fold_in(own_key, axis), (), 0, dims[axis]) for axis in range(len(dims))]
    array = array.at[tuple(place)].set(low)
    longest = dims.index(max(dims))
    place[longest] = (place[longest] + 1) % dims[longest]
    return array.at[tuple(place)].set(high)


def levels(rng, dims, pieces, least, top_value):
    level, own = 1.0, jax.random.fold_in(rng, 6)
    for position, blocks in pieces:
        steps = jnp.exp(jax.random.uniform(jax.random.fold_in(own, position), (blocks,), jnp.float32, least / len(pieces), top_value / len(pieces)))
        level = level * jnp.repeat(steps, dims[position] // blocks).reshape([-1 if axis == position else 1 for axis in range(len(dims))])
    return level


def rank_table(number_of, lean):
    portions = [(1 << 20) // math.isqrt(standing ** lean) + 1 for standing in range(1, number_of + 1)]
    deviation = 1 + sum(portions) // (1 << 30)
    return np.cumsum(np.array([max(1, weight // deviation) for weight in portions]))


def ranked(rng, dims, count, slope):
    table = rank_table(count, slope)
    ticket = jax.random.randint(jax.random.fold_in(rng, 1), dims, 0, int(table[count - 1]))
    grade = jnp.searchsorted(jnp.asarray(table, jnp.int32), ticket, side="right")
    return jax.random.permutation(jax.random.fold_in(rng, 2), count)[grade].astype(jnp.int32)


def normal_values(key, shape, spread, most, cuts=(), dtype=jnp.bfloat16):
    drawn = jax.random.normal(key, shape, jnp.float32) * spread
    if len(cuts) > 0:
        drawn = levels(key, shape, cuts, -0.22, 0.18) * drawn
    return jnp.clip(drawn, min=-most, max=most).astype(dtype)


def setup_inputs(seed: int = 0, part: int = 0) -> dict:
    arg_keys = jax.random.split(jax.random.key(seed), 9)
    part_splits = jax.random.split(jax.random.fold_in(arg_keys[8], part), 9)
    return {
        "input_after_norm": normal_values(part_splits[0], (TOKENS, MODEL_WIDTH), 1.0, 6.0, ((0, 32),)),
        "value_cotangent": normal_values(part_splits[1], (TOKENS, VALUE_WIDTH), 1.0, 6.0, ((0, 32),)),
        "value_weight": normal_values(arg_keys[2], (MODEL_WIDTH, VALUE_WIDTH), MODEL_WIDTH ** -0.5, 0.078125, ((0, 32),)),
        "down_factors": normal_values(arg_keys[3], (MODEL_WIDTH, ADAPTER_COUNT * ADAPTER_RANK), MODEL_WIDTH ** -0.5, 0.078125, ((0, 32),)),
        "up_factors": normal_values(arg_keys[4], (ADAPTER_COUNT * ADAPTER_RANK, VALUE_WIDTH), VALUE_WIDTH ** -0.5, 0.1875, ((0, 32),)),
        "sequence_adapter": with_ends(ranked(part_splits[5], (SEQS,), ADAPTER_COUNT, 2), jax.random.fold_in(part_splits[5], 3), 0, ADAPTER_COUNT - 1).astype(jnp.int32),
        "sequence_loss_length": with_ends(jax.random.randint(part_splits[6], (SEQS,), LENGTH // 4, LENGTH + 1), jax.random.fold_in(part_splits[6], 1), LENGTH // 4, LENGTH).astype(jnp.int32),
        "adapter_owner_slot": jax.random.permutation(arg_keys[7], ADAPTER_COUNT).astype(jnp.int32),
    }


adapter_scale = 2.0


def reference(input_after_norm, value_cotangent, value_weight, down_factors, up_factors, sequence_adapter, sequence_loss_length, adapter_owner_slot):
    positions = jnp.arange(LENGTH)
    x_seq = input_after_norm.reshape(SEQS, LENGTH, MODEL_WIDTH)
    dv_seq = value_cotangent.reshape(SEQS, LENGTH, VALUE_WIDTH)
    down_columns = down_factors.reshape(MODEL_WIDTH, ADAPTER_COUNT, ADAPTER_RANK)
    up_rows = up_factors.reshape(ADAPTER_COUNT, ADAPTER_RANK, VALUE_WIDTH)

    def one(carry, inputs):
        acc_a, acc_b = carry
        x_one, dv_raw, adapter_id, size = inputs
        value_grad_single = jnp.where((positions < size)[:, None], dv_raw, jnp.zeros_like(dv_raw))
        slot = adapter_owner_slot[adapter_id]
        a_sel = lax.dynamic_index_in_dim(down_columns, adapter_id, 1, keepdims=False)
        up_selected = lax.dynamic_index_in_dim(up_rows, slot, 0, keepdims=False)
        base_term = jnp.dot(value_grad_single, value_weight.T, preferred_element_type=jnp.float32)
        low_rank_gradient = (adapter_scale * jnp.dot(value_grad_single, up_selected.T, preferred_element_type=jnp.float32)).astype(jnp.bfloat16)
        d_one = (base_term + jnp.dot(low_rank_gradient, a_sel.T, preferred_element_type=jnp.float32)).astype(jnp.bfloat16)
        low_rank_update = jnp.dot(x_one, a_sel, preferred_element_type=jnp.float32).astype(jnp.bfloat16)
        part_a = jnp.dot(x_one.T, low_rank_gradient, preferred_element_type=jnp.float32)
        up_piece = adapter_scale * jnp.dot(low_rank_update.T, value_grad_single, preferred_element_type=jnp.float32)
        old_a = lax.dynamic_index_in_dim(acc_a, adapter_id, 1, keepdims=True)
        acc_a = lax.dynamic_update_index_in_dim(acc_a, old_a + part_a[:, None, :], adapter_id, 1)
        old_b = lax.dynamic_index_in_dim(acc_b, slot, 0, keepdims=True)
        acc_b = lax.dynamic_update_index_in_dim(acc_b, old_b + up_piece[None], slot, 0)
        return (acc_a, acc_b), d_one

    start = (jnp.zeros((MODEL_WIDTH, ADAPTER_COUNT, ADAPTER_RANK), jnp.float32), jnp.zeros((ADAPTER_COUNT, ADAPTER_RANK, VALUE_WIDTH), jnp.float32))
    (acc_a, acc_b), d_seq = lax.scan(one, start, (x_seq, dv_seq, sequence_adapter, sequence_loss_length))
    return d_seq.reshape(TOKENS, MODEL_WIDTH), acc_a.reshape(MODEL_WIDTH, ADAPTER_COUNT * ADAPTER_RANK), acc_b.reshape(ADAPTER_COUNT * ADAPTER_RANK, VALUE_WIDTH)
```

```python
import functools

import jax
import jax.numpy as jnp
from jax import lax
from jax.experimental import pallas as pl
from jax.experimental.pallas import tpu as pltpu
from jax.sharding import PartitionSpec as P

RANK = 16
LANES = 128
SCALE = 2.0
BF16 = jnp.bfloat16
F32 = jnp.float32
CONTRACT_LANES = (((1,), (1,)), ((), ()))
CONTRACT_ROWS = (((0,), (0,)), ((), ()))
CONTRACT_INNER = (((1,), (0,)), ((), ()))
VMEM = pl.BlockSpec(memory_space=pltpu.VMEM)
SMEM = pl.BlockSpec(memory_space=pltpu.SMEM)


def dot(a, b, dims):
    return lax.dot_general(a, b, dims, preferred_element_type=F32)


def params(megabytes):
    return pltpu.CompilerParams(vmem_limit_bytes=megabytes << 20)


def selectors(met_ref, slots_ref, id_lane):
    rows = met_ref.shape[0]
    adapter = met_ref[:, id_lane:id_lane + 1].astype(F32).astype(jnp.int32)
    lane = lax.broadcasted_iota(jnp.int32, (rows, slots_ref.shape[1]), 1)
    slot = jnp.sum(jnp.where(lane == adapter, slots_ref[...], 0).astype(F32), axis=1, keepdims=True)
    slot = slot.astype(jnp.int32)
    column = lax.broadcasted_iota(jnp.int32, (rows, rows), 1)
    rank = lax.broadcasted_iota(jnp.int32, (rows, 1), 0) % RANK
    by_adapter = jnp.where(column == adapter * RANK + rank, 1.0, 0.0).astype(BF16)
    by_slot = jnp.where(column == slot * RANK + rank, 1.0, 0.0).astype(BF16)
    return by_adapter, by_slot


def pick_kernel(chunk, met_ref, down_ref, slots_ref, out_ref):
    by_adapter, by_slot = selectors(met_ref, slots_ref, chunk)
    rows = down_ref.shape[0]
    out_ref[:, :rows] = dot(by_adapter, down_ref[...], CONTRACT_LANES).astype(BF16)
    picked = dot(by_slot, met_ref[...], CONTRACT_INNER).astype(BF16)
    out_ref[:, rows:rows + chunk] = picked[:, :chunk]


def place_kernel(chunk, met_ref, slots_ref, sums_ref, down_ref, up_ref):
    by_adapter, by_slot = selectors(met_ref, slots_ref, chunk)
    rows = down_ref.shape[0]
    down_ref[...] = dot(sums_ref[:, :rows], by_adapter, CONTRACT_ROWS)
    up_ref[...] = dot(by_slot, sums_ref[:, rows:rows + chunk], CONTRACT_ROWS)


def masked(dv, length):
    position = lax.broadcasted_iota(jnp.int32, (dv.shape[0], 1), 0)
    return jnp.where(position < length, dv, jnp.zeros_like(dv))


def rank_kernel(rows, chunk, length_ref, x_ref, dv_ref, got_ref, down_ref, g_ref, out_ref, up_ref):
    devices = got_ref.shape[0]
    for j in range(devices):
        down_ref[:, j * rows:(j + 1) * rows] = got_ref[j, :, :rows]
        up_ref[:, j * chunk:(j + 1) * chunk] = got_ref[j, :, rows:rows + chunk]
    dv = masked(dv_ref[...], length_ref[0])
    g = (SCALE * dot(up_ref[...], dv, CONTRACT_LANES)).astype(BF16)
    g_ref[...] = g
    u = dot(down_ref[...], x_ref[...], CONTRACT_LANES).astype(BF16)
    down_sum = dot(g, x_ref[...], CONTRACT_INNER).astype(BF16)
    up_sum = (SCALE * dot(u, dv, CONTRACT_INNER)).astype(BF16)
    for j in range(devices):
        out_ref[j, :, :rows] = down_sum[:, j * rows:(j + 1) * rows]
        out_ref[j, :, rows:rows + chunk] = up_sum[:, j * chunk:(j + 1) * chunk]


def product_kernel(length_ref, dv_ref, g_ref, w_ref, down_ref, out_ref):
    dv = masked(dv_ref[...], length_ref[0])
    base = dot(dv, w_ref[...], CONTRACT_LANES)
    out_ref[...] = (base + dot(g_ref[...], down_ref[...], CONTRACT_ROWS)).astype(BF16)


def local(x, dv, weight, down, up, sequence_adapter, loss_length, owner_slot):
    devices = lax.axis_size("dp")
    tokens, width = x.shape
    value = dv.shape[1]
    rows = down.shape[0]
    chunk = value // devices
    ranks = devices * RANK
    slots = owner_slot.reshape(1, devices)

    weights = lax.all_gather(weight, "dp", axis=0, tiled=True)

    own_up = up.reshape(RANK, devices, chunk).transpose(1, 0, 2)
    own_id = jnp.broadcast_to(sequence_adapter.astype(BF16).reshape(1, 1, 1), (devices, RANK, 1))
    first = jnp.concatenate([own_up, own_id, jnp.zeros((devices, RANK, LANES - 1 - chunk), BF16)], axis=2)
    met = lax.all_to_all(first, "dp", split_axis=0, concat_axis=0, tiled=True).reshape(ranks, LANES)

    second = pl.pallas_call(
        functools.partial(pick_kernel, chunk),
        out_shape=jax.ShapeDtypeStruct((ranks, rows + chunk), BF16),
        in_specs=[VMEM, VMEM, VMEM],
        out_specs=VMEM,
        compiler_params=params(48),
    )(met, down, slots)
    got = lax.all_to_all(second.reshape(devices, RANK, rows + chunk), "dp", split_axis=0, concat_axis=0, tiled=True)

    own_down, g, third = pl.pallas_call(
        functools.partial(rank_kernel, rows, chunk),
        out_shape=(
            jax.ShapeDtypeStruct((RANK, width), BF16),
            jax.ShapeDtypeStruct((RANK, tokens), BF16),
            jax.ShapeDtypeStruct((devices, RANK, rows + chunk), BF16),
        ),
        in_specs=[SMEM, VMEM, VMEM, VMEM],
        out_specs=(VMEM, VMEM, VMEM),
        scratch_shapes=[pltpu.VMEM((RANK, value), BF16)],
        compiler_params=params(48),
    )(loss_length, x, dv, got)
    sums = lax.all_to_all(third, "dp", split_axis=0, concat_axis=0, tiled=True).reshape(ranks, rows + chunk)

    grad_down, slot_sums = pl.pallas_call(
        functools.partial(place_kernel, chunk),
        out_shape=(jax.ShapeDtypeStruct((rows, ranks), F32), jax.ShapeDtypeStruct((ranks, chunk), F32)),
        in_specs=[VMEM, VMEM, VMEM],
        out_specs=(VMEM, VMEM),
        compiler_params=params(48),
    )(met, slots, sums)
    fourth = lax.all_to_all(slot_sums.reshape(devices, RANK, chunk), "dp", split_axis=0, concat_axis=0, tiled=True)
    grad_up = fourth.transpose(1, 0, 2).reshape(RANK, value)

    tile = 640
    grad_x = pl.pallas_call(
        product_kernel,
        out_shape=jax.ShapeDtypeStruct((tokens, width), BF16),
        grid=(width // tile,),
        in_specs=[
            SMEM,
            pl.BlockSpec((tokens, value), lambda i: (0, 0)),
            pl.BlockSpec((RANK, tokens), lambda i: (0, 0)),
            pl.BlockSpec((tile, value), lambda i: (i, 0)),
            pl.BlockSpec((RANK, tile), lambda i: (0, i)),
        ],
        out_specs=pl.BlockSpec((tokens, tile), lambda i: (0, i)),
        compiler_params=params(48),
    )(loss_length, dv, g, weights, own_down)
    return grad_x, grad_down, grad_up


def solution(mesh):
    split = P(("groups", "dp"))
    rows = P(("groups", "dp"), None)
    shard = P("dp", None)
    return jax.shard_map(
        local,
        mesh=mesh,
        in_specs=(rows, rows, shard, shard, shard, split, split, P()),
        out_specs=(rows, rows, rows),
        check_vma=False,
    )
```

```python
import functools

import jax
import jax.numpy as jnp
from jax import lax
from jax.experimental import pallas as pl
from jax.experimental.pallas import tpu as pltpu
from jax.sharding import PartitionSpec as P

RANK = 16
LANES = 128
SCALE = 2.0
BF16 = jnp.bfloat16
F32 = jnp.float32
CONTRACT_LANES = (((1,), (1,)), ((), ()))
CONTRACT_ROWS = (((0,), (0,)), ((), ()))
CONTRACT_INNER = (((1,), (0,)), ((), ()))
VMEM = pl.BlockSpec(memory_space=pltpu.VMEM)
ANY = pl.BlockSpec(memory_space=pl.ANY)
SMEM = pl.BlockSpec(memory_space=pltpu.SMEM)


def dot(a, b, dims):
    return lax.dot_general(a, b, dims, preferred_element_type=F32)


def params(megabytes):
    return pltpu.CompilerParams(vmem_limit_bytes=megabytes << 20)


def selectors(met_ref, slots_ref, id_lane):
    rows = met_ref.shape[0]
    adapter = met_ref[:, id_lane:id_lane + 1].astype(F32).astype(jnp.int32)
    lane = lax.broadcasted_iota(jnp.int32, (rows, slots_ref.shape[1]), 1)
    slot = jnp.sum(jnp.where(lane == adapter, slots_ref[...], 0).astype(F32), axis=1, keepdims=True)
    slot = slot.astype(jnp.int32)
    column = lax.broadcasted_iota(jnp.int32, (rows, rows), 1)
    rank = lax.broadcasted_iota(jnp.int32, (rows, 1), 0) % RANK
    by_adapter = jnp.where(column == adapter * RANK + rank, 1.0, 0.0).astype(BF16)
    by_slot = jnp.where(column == slot * RANK + rank, 1.0, 0.0).astype(BF16)
    return by_adapter, by_slot


def pick_kernel(chunk, met_ref, down_ref, slots_ref, out_ref):
    by_adapter, by_slot = selectors(met_ref, slots_ref, chunk)
    rows = down_ref.shape[0]
    out_ref[:, :rows] = dot(by_adapter, down_ref[...], CONTRACT_LANES).astype(BF16)
    picked = dot(by_slot, met_ref[...], CONTRACT_INNER).astype(BF16)
    out_ref[:, rows:rows + chunk] = picked[:, :chunk]


def place_kernel(chunk, met_ref, slots_ref, sums_ref, down_ref, up_ref):
    by_adapter, by_slot = selectors(met_ref, slots_ref, chunk)
    rows = down_ref.shape[0]
    down_ref[...] = dot(sums_ref[:, :rows], by_adapter, CONTRACT_ROWS)
    up_ref[...] = dot(by_slot, sums_ref[:, rows:rows + chunk], CONTRACT_ROWS)


def masked(dv, length):
    position = lax.broadcasted_iota(jnp.int32, (dv.shape[0], 1), 0)
    return jnp.where(position < length, dv, jnp.zeros_like(dv))


def rank_kernel(rows, chunk, length_ref, x_ref, dv_ref, got_ref, down_ref, g_ref, out_ref, up_ref):
    devices = got_ref.shape[0]
    for j in range(devices):
        down_ref[:, j * rows:(j + 1) * rows] = got_ref[j, :, :rows]
        up_ref[:, j * chunk:(j + 1) * chunk] = got_ref[j, :, rows:rows + chunk]
    dv = masked(dv_ref[...], length_ref[0])
    g = (SCALE * dot(up_ref[...], dv, CONTRACT_LANES)).astype(BF16)
    g_ref[...] = g
    u = dot(down_ref[...], x_ref[...], CONTRACT_LANES).astype(BF16)
    down_sum = dot(g, x_ref[...], CONTRACT_INNER).astype(BF16)
    up_sum = (SCALE * dot(u, dv, CONTRACT_INNER)).astype(BF16)
    for j in range(devices):
        out_ref[j, :, :rows] = down_sum[:, j * rows:(j + 1) * rows]
        out_ref[j, :, rows:rows + chunk] = up_sum[:, j * chunk:(j + 1) * chunk]


def product_kernel(half_ref, length_ref, dv_ref, g_ref, w_ref, down_ref, *refs):
    dv = masked(dv_ref[...], length_ref[0])
    base = dot(dv, w_ref[...], CONTRACT_LANES)
    refs[-1][...] = (base + dot(g_ref[...], down_ref[...], CONTRACT_ROWS)).astype(BF16)


def exchange(value):
    return lax.all_to_all(value, "dp", split_axis=0, concat_axis=0, tiled=True)


def local(x, dv, weight, down, up, sequence_adapter, loss_length, owner_slot):
    devices = lax.axis_size("dp")
    tokens, width = x.shape
    value = dv.shape[1]
    rows = down.shape[0]
    chunk = value // devices
    ranks = devices * RANK
    slots = owner_slot.reshape(1, devices)

    half = devices // 2
    my_half = (lax.axis_index("dp") // half).astype(jnp.int32)
    sides = [list(range(half)), list(range(half, devices))]
    far_shard = lax.ppermute(weight, "dp", [(i, i ^ half) for i in range(devices)])
    near_weight = lax.all_gather(weight, "dp", axis=0, tiled=True, axis_index_groups=sides)
    far_weight = lax.all_gather(far_shard, "dp", axis=0, tiled=True, axis_index_groups=sides)

    own_up = up.reshape(RANK, devices, chunk).transpose(1, 0, 2)
    own_id = jnp.broadcast_to(sequence_adapter.astype(BF16).reshape(1, 1, 1), (devices, RANK, 1))
    first = jnp.concatenate([own_up, own_id, jnp.zeros((devices, RANK, LANES - 1 - chunk), BF16)], axis=2)
    met = exchange(first).reshape(ranks, LANES)

    second = pl.pallas_call(
        functools.partial(pick_kernel, chunk),
        out_shape=jax.ShapeDtypeStruct((ranks, rows + chunk), BF16),
        in_specs=[VMEM, VMEM, VMEM],
        out_specs=VMEM,
        compiler_params=params(8),
    )(met, down, slots)
    got = exchange(second.reshape(devices, RANK, rows + chunk))

    own_down, g, third = pl.pallas_call(
        functools.partial(rank_kernel, rows, chunk),
        out_shape=(
            jax.ShapeDtypeStruct((RANK, width), BF16),
            jax.ShapeDtypeStruct((RANK, tokens), BF16),
            jax.ShapeDtypeStruct((devices, RANK, rows + chunk), BF16),
        ),
        in_specs=[SMEM, VMEM, VMEM, VMEM],
        out_specs=(VMEM, VMEM, VMEM),
        scratch_shapes=[pltpu.VMEM((RANK, value), BF16)],
        compiler_params=params(8),
    )(loss_length, x, dv, got)
    sums = exchange(third).reshape(ranks, rows + chunk)

    grad_down, slot_sums = pl.pallas_call(
        functools.partial(place_kernel, chunk),
        out_shape=(jax.ShapeDtypeStruct((rows, ranks), F32), jax.ShapeDtypeStruct((ranks, chunk), F32)),
        in_specs=[VMEM, VMEM, VMEM],
        out_specs=(VMEM, VMEM),
        compiler_params=params(8),
    )(met, slots, sums)
    fourth = exchange(slot_sums.reshape(devices, RANK, chunk))
    grad_up = fourth.transpose(1, 0, 2).reshape(RANK, value)

    steps = 2
    tile = width // (2 * steps)

    def product(half, weights, *earlier):
        def here(i, half):
            return 0, half[0] * steps + i

        return pl.pallas_call(
            product_kernel,
            out_shape=jax.ShapeDtypeStruct((tokens, width), BF16),
            grid_spec=pltpu.PrefetchScalarGridSpec(
                num_scalar_prefetch=1,
                grid=(steps,),
                in_specs=[
                    SMEM,
                    pl.BlockSpec((tokens, value), lambda i, half: (0, 0)),
                    pl.BlockSpec((RANK, tokens), lambda i, half: (0, 0)),
                    pl.BlockSpec((tile, value), lambda i, half: (i, 0)),
                    pl.BlockSpec((RANK, tile), here),
                ] + [ANY] * len(earlier),
                out_specs=pl.BlockSpec((tokens, tile), here),
            ),
            input_output_aliases={6: 0} if earlier else {},
            compiler_params=params(60),
        )(half.reshape(1), loss_length, dv, g, weights, own_down, *earlier)

    grad_x = product(1 - my_half, far_weight, product(my_half, near_weight))
    return grad_x, grad_down, grad_up


def solution(mesh):
    split = P(("groups", "dp"))
    rows = P(("groups", "dp"), None)
    shard = P("dp", None)
    return jax.shard_map(
        local,
        mesh=mesh,
        in_specs=(rows, rows, shard, shard, shard, split, split, P()),
        out_specs=(rows, rows, rows),
        check_vma=False,
    )
```

```python
import functools

import jax
import jax.numpy as jnp
from jax import lax
from jax.experimental import pallas as pl
from jax.experimental.pallas import tpu as pltpu
from jax.sharding import PartitionSpec as P

RANK = 16
LANES = 128
SCALE = 2.0
BF16 = jnp.bfloat16
F32 = jnp.float32
CONTRACT_LANES = (((1,), (1,)), ((), ()))
CONTRACT_ROWS = (((0,), (0,)), ((), ()))
CONTRACT_INNER = (((1,), (0,)), ((), ()))
VMEM = pl.BlockSpec(memory_space=pltpu.VMEM)
HBM = pl.BlockSpec(memory_space=pltpu.HBM)
SMEM = pl.BlockSpec(memory_space=pltpu.SMEM)


def dot(a, b, dims):
    return lax.dot_general(a, b, dims, preferred_element_type=F32)


def params(megabytes):
    return pltpu.CompilerParams(vmem_limit_bytes=megabytes << 20)


def selectors(met_ref, slots_ref, id_lane):
    rows = met_ref.shape[0]
    adapter = met_ref[:, id_lane:id_lane + 1].astype(F32).astype(jnp.int32)
    lane = lax.broadcasted_iota(jnp.int32, (rows, slots_ref.shape[1]), 1)
    slot = jnp.sum(jnp.where(lane == adapter, slots_ref[...], 0).astype(F32), axis=1, keepdims=True)
    slot = slot.astype(jnp.int32)
    column = lax.broadcasted_iota(jnp.int32, (rows, rows), 1)
    rank = lax.broadcasted_iota(jnp.int32, (rows, 1), 0) % RANK
    by_adapter = jnp.where(column == adapter * RANK + rank, 1.0, 0.0).astype(BF16)
    by_slot = jnp.where(column == slot * RANK + rank, 1.0, 0.0).astype(BF16)
    return by_adapter, by_slot


def pick_kernel(chunk, met_ref, down_ref, slots_ref, out_ref):
    by_adapter, by_slot = selectors(met_ref, slots_ref, chunk)
    rows = down_ref.shape[0]
    out_ref[:, :rows] = dot(by_adapter, down_ref[...], CONTRACT_LANES).astype(BF16)
    picked = dot(by_slot, met_ref[...], CONTRACT_INNER).astype(BF16)
    out_ref[:, rows:rows + chunk] = picked[:, :chunk]


def place_kernel(chunk, met_ref, slots_ref, sums_ref, down_ref, up_ref):
    by_adapter, by_slot = selectors(met_ref, slots_ref, chunk)
    rows = down_ref.shape[0]
    down_ref[...] = dot(sums_ref[:, :rows], by_adapter, CONTRACT_ROWS)
    up_ref[...] = dot(by_slot, sums_ref[:, rows:rows + chunk], CONTRACT_ROWS)


def masked(dv, length):
    position = lax.broadcasted_iota(jnp.int32, (dv.shape[0], 1), 0)
    return jnp.where(position < length, dv, jnp.zeros_like(dv))


def rank_kernel(rows, chunk, length_ref, x_ref, dv_ref, got_ref, down_ref, g_ref, out_ref, up_ref):
    devices = got_ref.shape[0]
    for j in range(devices):
        down_ref[:, j * rows:(j + 1) * rows] = got_ref[j, :, :rows]
        up_ref[:, j * chunk:(j + 1) * chunk] = got_ref[j, :, rows:rows + chunk]
    dv = masked(dv_ref[...], length_ref[0])
    g = (SCALE * dot(up_ref[...], dv, CONTRACT_LANES)).astype(BF16)
    g_ref[...] = g
    u = dot(down_ref[...], x_ref[...], CONTRACT_LANES).astype(BF16)
    down_sum = dot(g, x_ref[...], CONTRACT_INNER).astype(BF16)
    up_sum = (SCALE * dot(u, dv, CONTRACT_INNER)).astype(BF16)
    for j in range(devices):
        out_ref[j, :, :rows] = down_sum[:, j * rows:(j + 1) * rows]
        out_ref[j, :, rows:rows + chunk] = up_sum[:, j * chunk:(j + 1) * chunk]


def product_kernel(order, length_ref, dv_ref, g_ref, down_ref, w_ref, out_ref, held_ref, block_ref, sem, out_sem):
    groups, places, rows, _ = held_ref.shape
    copies = [[] for _ in range(groups)]
    for position, block in enumerate(order):
        source = w_ref.at[pl.ds(position * rows, rows)]
        group, place = block // places, block % places
        copies[group].append(pltpu.make_async_copy(source, held_ref.at[group, place], sem.at[group, place]))

    def leave(group):
        target = out_ref.at[:, pl.ds(group * places * rows, places * rows)]
        return pltpu.make_async_copy(block_ref.at[group], target, out_sem.at[group])

    for group in copies:
        for copy in group:
            copy.start()
    dv = masked(dv_ref[...], length_ref[0])
    for group in range(groups):
        for copy in copies[group]:
            copy.wait()
        weight = held_ref[group].reshape(places * rows, dv.shape[1])
        columns = slice(group * places * rows, (group + 1) * places * rows)
        total = dot(dv, weight, CONTRACT_LANES) + dot(g_ref[...], down_ref[:, columns], CONTRACT_ROWS)
        block_ref[group] = total.astype(BF16)
        leave(group).start()
    for group in range(groups):
        leave(group).wait()


def snake(sizes):
    path = [0]
    for size in sizes:
        path = [i * size + k for at, i in enumerate(path) for k in (range(size) if at % 2 == 0 else reversed(range(size)))]
    return path


def exchange(value):
    return lax.all_to_all(value, "dp", split_axis=0, concat_axis=0, tiled=True)


def local(x, dv, weight, down, up, sequence_adapter, loss_length, owner_slot):
    devices = lax.axis_size("dp")
    tokens, width = x.shape
    value = dv.shape[1]
    rows = down.shape[0]
    chunk = value // devices
    ranks = devices * RANK
    slots = owner_slot.reshape(1, devices)

    chips = devices // 2
    side = int(chips ** 0.5)
    path = snake((chips // 4, 2, 2) if chips <= 16 else (side, chips // side))
    ring = [2 * chip + core for chip in path for core in range(2)]
    weights = lax.all_gather(weight, "dp", axis=0, tiled=True, axis_index_groups=[ring])

    own_up = up.reshape(RANK, devices, chunk).transpose(1, 0, 2)
    own_id = jnp.broadcast_to(sequence_adapter.astype(BF16).reshape(1, 1, 1), (devices, RANK, 1))
    first = jnp.concatenate([own_up, own_id, jnp.zeros((devices, RANK, LANES - 1 - chunk), BF16)], axis=2)
    met = exchange(first).reshape(ranks, LANES)

    second = pl.pallas_call(
        functools.partial(pick_kernel, chunk),
        out_shape=jax.ShapeDtypeStruct((ranks, rows + chunk), BF16),
        in_specs=[VMEM, VMEM, VMEM],
        out_specs=VMEM,
        compiler_params=params(8),
    )(met, down, slots)
    got = exchange(second.reshape(devices, RANK, rows + chunk))

    own_down, g, third = pl.pallas_call(
        functools.partial(rank_kernel, rows, chunk),
        out_shape=(
            jax.ShapeDtypeStruct((RANK, width), BF16),
            jax.ShapeDtypeStruct((RANK, tokens), BF16),
            jax.ShapeDtypeStruct((devices, RANK, rows + chunk), BF16),
        ),
        in_specs=[SMEM, VMEM, VMEM, VMEM],
        out_specs=(VMEM, VMEM, VMEM),
        scratch_shapes=[pltpu.VMEM((RANK, value), BF16)],
        compiler_params=params(8),
    )(loss_length, x, dv, got)
    sums = exchange(third).reshape(ranks, rows + chunk)

    grad_down, slot_sums = pl.pallas_call(
        functools.partial(place_kernel, chunk),
        out_shape=(jax.ShapeDtypeStruct((rows, ranks), F32), jax.ShapeDtypeStruct((ranks, chunk), F32)),
        in_specs=[VMEM, VMEM, VMEM],
        out_specs=(VMEM, VMEM),
        compiler_params=params(8),
    )(met, slots, sums)
    fourth = exchange(slot_sums.reshape(devices, RANK, chunk))
    grad_up = fourth.transpose(1, 0, 2).reshape(RANK, value)

    order, block = path, 2 * rows
    if block % 16:
        back = sorted(range(chips), key=lambda position: path[position])
        weights = weights.reshape(chips, block, value)[jnp.array(back)].reshape(width, value)
    groups = 4
    if block % 16 or chips % groups:
        order, block = list(range(groups)), width // groups
    places = len(order) // groups
    grad_x = pl.pallas_call(
        functools.partial(product_kernel, order),
        out_shape=jax.ShapeDtypeStruct((tokens, width), BF16),
        in_specs=[SMEM, VMEM, VMEM, VMEM, HBM],
        out_specs=HBM,
        scratch_shapes=[
            pltpu.VMEM((groups, places, block, value), BF16),
            pltpu.VMEM((groups, tokens, places * block), BF16),
            pltpu.SemaphoreType.DMA((groups, places)),
            pltpu.SemaphoreType.DMA((groups,)),
        ],
        compiler_params=params(60),
    )(loss_length, dv, g, own_down, weights)
    return grad_x, grad_down, grad_up


def solution(mesh):
    split = P(("groups", "dp"))
    rows = P(("groups", "dp"), None)
    shard = P("dp", None)
    return jax.shard_map(
        local,
        mesh=mesh,
        in_specs=(rows, rows, shard, shard, shard, split, split, P()),
        out_specs=(rows, rows, rows),
        check_vma=False,
    )
```

```python
import functools

import jax
import jax.numpy as jnp
from jax import lax
from jax.experimental import pallas as pl
from jax.experimental.pallas import tpu as pltpu
from jax.sharding import PartitionSpec as P

RANK = 16
LANES = 128
COLUMNS = 256
SCALE = 2.0
BF16 = jnp.bfloat16
F32 = jnp.float32
CONTRACT_LANES = (((1,), (1,)), ((), ()))
CONTRACT_ROWS = (((0,), (0,)), ((), ()))
CONTRACT_INNER = (((1,), (0,)), ((), ()))
VMEM = pl.BlockSpec(memory_space=pltpu.VMEM)
HBM = pl.BlockSpec(memory_space=pltpu.HBM)
SMEM = pl.BlockSpec(memory_space=pltpu.SMEM)


def dot(a, b, dims):
    return lax.dot_general(a, b, dims, preferred_element_type=F32)


def params(megabytes):
    return pltpu.CompilerParams(vmem_limit_bytes=megabytes << 20)


def selectors(met_ref, slots_ref, id_lane):
    rows = met_ref.shape[0]
    adapter = met_ref[:, id_lane:id_lane + 1].astype(F32).astype(jnp.int32)
    lane = lax.broadcasted_iota(jnp.int32, (rows, slots_ref.shape[1]), 1)
    slot = jnp.sum(jnp.where(lane == adapter, slots_ref[...], 0).astype(F32), axis=1, keepdims=True)
    slot = slot.astype(jnp.int32)
    column = lax.broadcasted_iota(jnp.int32, (rows, rows), 1)
    rank = lax.broadcasted_iota(jnp.int32, (rows, 1), 0) % RANK
    by_adapter = jnp.where(column == adapter * RANK + rank, 1.0, 0.0).astype(BF16)
    by_slot = jnp.where(column == slot * RANK + rank, 1.0, 0.0).astype(BF16)
    return by_adapter, by_slot


def pick_kernel(chunk, met_ref, down_ref, slots_ref, out_ref):
    by_adapter, by_slot = selectors(met_ref, slots_ref, chunk)
    rows = down_ref.shape[0]
    out_ref[:, :rows] = dot(by_adapter, down_ref[...], CONTRACT_LANES).astype(BF16)
    picked = dot(by_slot, met_ref[...], CONTRACT_INNER).astype(BF16)
    out_ref[:, rows:rows + chunk] = picked[:, :chunk]


def place_kernel(chunk, met_ref, slots_ref, sums_ref, down_ref, up_ref):
    by_adapter, by_slot = selectors(met_ref, slots_ref, chunk)
    rows = down_ref.shape[0]
    down_ref[...] = dot(sums_ref[:, :rows], by_adapter, CONTRACT_ROWS)
    up_ref[...] = dot(by_slot, sums_ref[:, rows:rows + chunk], CONTRACT_ROWS)


def masked(dv, length):
    position = lax.broadcasted_iota(jnp.int32, (dv.shape[0], 1), 0)
    return jnp.where(position < length, dv, jnp.zeros_like(dv))


def rank_kernel(rows, chunk, length_ref, x_ref, dv_ref, got_ref, down_ref, g_ref, out_ref, up_ref):
    devices = got_ref.shape[0]
    for j in range(devices):
        down_ref[:, j * rows:(j + 1) * rows] = got_ref[j, :, :rows]
        up_ref[:, j * chunk:(j + 1) * chunk] = got_ref[j, :, rows:rows + chunk]
    dv = masked(dv_ref[...], length_ref[0])
    g = (SCALE * dot(up_ref[...], dv, CONTRACT_LANES)).astype(BF16)
    g_ref[...] = g
    u = dot(down_ref[...], x_ref[...], CONTRACT_LANES).astype(BF16)
    down_sum = dot(g, x_ref[...], CONTRACT_INNER).astype(BF16)
    up_sum = (SCALE * dot(u, dv, CONTRACT_INNER)).astype(BF16)
    for j in range(devices):
        out_ref[j, :, :rows] = down_sum[:, j * rows:(j + 1) * rows]
        out_ref[j, :, rows:rows + chunk] = up_sum[:, j * chunk:(j + 1) * chunk]


def product_kernel(order, length_ref, dv_ref, g_ref, down_ref, w_ref, out_ref, held_ref, block_ref, sem, out_sem):
    groups, places = sem.shape
    rows = held_ref.shape[1] // places
    copies = [[] for _ in range(groups)]
    for position, block in enumerate(order):
        source = w_ref.at[pl.ds(position * rows, rows)]
        group, place = block // places, block % places
        copies[group].append(pltpu.make_async_copy(source, held_ref.at[group, pl.ds(place * rows, rows)], sem.at[group, place]))

    def leave(group):
        target = out_ref.at[:, pl.ds(group * places * rows, places * rows)]
        return pltpu.make_async_copy(block_ref.at[group], target, out_sem.at[group])

    for group in copies:
        for copy in group:
            copy.start()
    dv = masked(dv_ref[...], length_ref[0])
    g = g_ref[...]
    for group in range(groups):
        for copy in copies[group]:
            copy.wait()
        for first in range(0, places * rows, COLUMNS):
            columns = slice(group * places * rows + first, group * places * rows + first + COLUMNS)
            total = dot(dv, held_ref[group, first:first + COLUMNS], CONTRACT_LANES)
            total += dot(g, down_ref[:, columns], CONTRACT_ROWS)
            block_ref[group, :, first:first + COLUMNS] = total.astype(BF16)
        leave(group).start()
    for group in range(groups):
        leave(group).wait()


def snake(sizes):
    path = [0]
    for size in sizes:
        path = [i * size + k for at, i in enumerate(path) for k in (range(size) if at % 2 == 0 else reversed(range(size)))]
    return path


def exchange(value):
    return lax.all_to_all(value, "dp", split_axis=0, concat_axis=0, tiled=True)


def local(x, dv, weight, down, up, sequence_adapter, loss_length, owner_slot):
    devices = lax.axis_size("dp")
    tokens, width = x.shape
    value = dv.shape[1]
    rows = down.shape[0]
    chunk = value // devices
    ranks = devices * RANK
    slots = owner_slot.reshape(1, devices)

    chips = devices // 2
    side = int(chips ** 0.5)
    path = snake((chips // 4, 2, 2) if chips <= 16 else (side, chips // side))
    ring = [2 * chip + core for chip in path for core in range(2)]
    weights = lax.all_gather(weight, "dp", axis=0, tiled=True, axis_index_groups=[ring])

    own_up = up.reshape(RANK, devices, chunk).transpose(1, 0, 2)
    own_id = jnp.broadcast_to(sequence_adapter.astype(BF16).reshape(1, 1, 1), (devices, 1, LANES))
    packed = jnp.concatenate([own_up.reshape(devices, -1, LANES), own_id], axis=1)
    met = exchange(packed)
    met_up = met[:, :-1].reshape(devices, RANK, chunk)
    met_id = jnp.broadcast_to(met[:, -1:, :LANES - chunk], (devices, RANK, LANES - chunk))
    met = jnp.concatenate([met_up, met_id], axis=2).reshape(ranks, LANES)

    second = pl.pallas_call(
        functools.partial(pick_kernel, chunk),
        out_shape=jax.ShapeDtypeStruct((ranks, rows + chunk), BF16),
        in_specs=[VMEM, VMEM, VMEM],
        out_specs=VMEM,
        compiler_params=params(8),
    )(met, down, slots)
    got = exchange(second.reshape(devices, -1, LANES)).reshape(devices, RANK, rows + chunk)

    own_down, g, third = pl.pallas_call(
        functools.partial(rank_kernel, rows, chunk),
        out_shape=(
            jax.ShapeDtypeStruct((RANK, width), BF16),
            jax.ShapeDtypeStruct((RANK, tokens), BF16),
            jax.ShapeDtypeStruct((devices, RANK, rows + chunk), BF16),
        ),
        in_specs=[SMEM, VMEM, VMEM, VMEM],
        out_specs=(VMEM, VMEM, VMEM),
        scratch_shapes=[pltpu.VMEM((RANK, value), BF16)],
        compiler_params=params(8),
    )(loss_length, x, dv, got)
    sums = exchange(third.reshape(devices, -1, LANES)).reshape(ranks, rows + chunk)

    grad_down, slot_sums = pl.pallas_call(
        functools.partial(place_kernel, chunk),
        out_shape=(jax.ShapeDtypeStruct((rows, ranks), F32), jax.ShapeDtypeStruct((ranks, chunk), F32)),
        in_specs=[VMEM, VMEM, VMEM],
        out_specs=(VMEM, VMEM),
        compiler_params=params(8),
    )(met, slots, sums)
    fourth = exchange(slot_sums.reshape(devices, RANK, chunk))
    grad_up = fourth.transpose(1, 0, 2).reshape(RANK, value)

    order, block = path, 2 * rows
    if block % 16:
        back = sorted(range(chips), key=lambda position: path[position])
        weights = weights.reshape(chips, block, value)[jnp.array(back)].reshape(width, value)
    groups = 4
    if block % 16 or chips % groups:
        order, block = list(range(groups)), width // groups
    places = len(order) // groups
    grad_x = pl.pallas_call(
        functools.partial(product_kernel, order),
        out_shape=jax.ShapeDtypeStruct((tokens, width), BF16),
        in_specs=[SMEM, VMEM, VMEM, VMEM, HBM],
        out_specs=HBM,
        scratch_shapes=[
            pltpu.VMEM((groups, places * block, value), BF16),
            pltpu.VMEM((groups, tokens, places * block), BF16),
            pltpu.SemaphoreType.DMA((groups, places)),
            pltpu.SemaphoreType.DMA((groups,)),
        ],
        compiler_params=params(60),
    )(loss_length, dv, g, own_down, weights)
    return grad_x, grad_down, grad_up


def solution(mesh):
    split = P(("groups", "dp"))
    rows = P(("groups", "dp"), None)
    shard = P("dp", None)
    return jax.shard_map(
        local,
        mesh=mesh,
        in_specs=(rows, rows, shard, shard, shard, split, split, P()),
        out_specs=(rows, rows, rows),
        check_vma=False,
    )
```

```python
import functools

import jax
import jax.numpy as jnp
from jax import lax
from jax.experimental import pallas as pl
from jax.experimental.pallas import tpu as pltpu
from jax.sharding import PartitionSpec as P

RANK = 16
LANES = 128
COLUMNS = 512
SCALE = 2.0
BF16 = jnp.bfloat16
F32 = jnp.float32
CONTRACT_LANES = (((1,), (1,)), ((), ()))
CONTRACT_ROWS = (((0,), (0,)), ((), ()))
CONTRACT_INNER = (((1,), (0,)), ((), ()))
VMEM = pl.BlockSpec(memory_space=pltpu.VMEM)
HBM = pl.BlockSpec(memory_space=pltpu.HBM)
SMEM = pl.BlockSpec(memory_space=pltpu.SMEM)


def dot(a, b, dims):
    return lax.dot_general(a, b, dims, preferred_element_type=F32)


def params(megabytes):
    return pltpu.CompilerParams(vmem_limit_bytes=megabytes << 20)


def selectors(met_ref, slots_ref, id_lane):
    rows = met_ref.shape[0]
    adapter = met_ref[:, id_lane:id_lane + 1].astype(F32).astype(jnp.int32)
    lane = lax.broadcasted_iota(jnp.int32, (rows, slots_ref.shape[1]), 1)
    slot = jnp.sum(jnp.where(lane == adapter, slots_ref[...], 0).astype(F32), axis=1, keepdims=True)
    slot = slot.astype(jnp.int32)
    column = lax.broadcasted_iota(jnp.int32, (rows, rows), 1)
    rank = lax.broadcasted_iota(jnp.int32, (rows, 1), 0) % RANK
    by_adapter = jnp.where(column == adapter * RANK + rank, 1.0, 0.0).astype(BF16)
    by_slot = jnp.where(column == slot * RANK + rank, 1.0, 0.0).astype(BF16)
    return by_adapter, by_slot


def pick_kernel(chunk, met_ref, down_ref, slots_ref, out_ref):
    by_adapter, by_slot = selectors(met_ref, slots_ref, chunk)
    rows = down_ref.shape[0]
    out_ref[:, :rows] = dot(by_adapter, down_ref[...], CONTRACT_LANES).astype(BF16)
    picked = dot(by_slot, met_ref[...], CONTRACT_INNER).astype(BF16)
    out_ref[:, rows:rows + chunk] = picked[:, :chunk]


def place_kernel(chunk, met_ref, slots_ref, sums_ref, down_ref, up_ref):
    by_adapter, by_slot = selectors(met_ref, slots_ref, chunk)
    rows = down_ref.shape[0]
    down_ref[...] = dot(sums_ref[:, :rows], by_adapter, CONTRACT_ROWS)
    up_ref[...] = dot(by_slot, sums_ref[:, rows:rows + chunk], CONTRACT_ROWS)


def masked(dv, length):
    position = lax.broadcasted_iota(jnp.int32, (dv.shape[0], 1), 0)
    return jnp.where(position < length, dv, jnp.zeros_like(dv))


def rank_kernel(rows, chunk, length_ref, x_ref, dv_ref, got_ref, down_ref, g_ref, out_ref, up_ref):
    devices = got_ref.shape[0]
    for j in range(devices):
        down_ref[:, j * rows:(j + 1) * rows] = got_ref[j, :, :rows]
        up_ref[:, j * chunk:(j + 1) * chunk] = got_ref[j, :, rows:rows + chunk]
    dv = masked(dv_ref[...], length_ref[0])
    g = (SCALE * dot(up_ref[...], dv, CONTRACT_LANES)).astype(BF16)
    g_ref[...] = g
    u = dot(down_ref[...], x_ref[...], CONTRACT_LANES).astype(BF16)
    down_sum = dot(g, x_ref[...], CONTRACT_INNER).astype(BF16)
    up_sum = (SCALE * dot(u, dv, CONTRACT_INNER)).astype(BF16)
    for j in range(devices):
        out_ref[j, :, :rows] = down_sum[:, j * rows:(j + 1) * rows]
        out_ref[j, :, rows:rows + chunk] = up_sum[:, j * chunk:(j + 1) * chunk]


def product_kernel(order, length_ref, dv_ref, g_ref, down_ref, w_ref, out_ref, *scratch):
    held, columns, sem, out_sem = scratch
    rows = held.shape[0] // len(order)
    copies = [None] * len(order)
    for position, block in enumerate(order):
        source = w_ref.at[pl.ds(position * rows, rows)]
        copies[block] = pltpu.make_async_copy(source, held.at[pl.ds(block * rows, rows)], sem.at[block])
    for copy in copies:
        copy.start()
    dv = masked(dv_ref[...], length_ref[0])
    g = g_ref[...]
    groups = out_sem.shape[0]
    leaving = []
    done = 0
    for group in range(groups):
        here = len(order) * (group + 1) // groups
        for copy in copies[len(order) * group // groups:here]:
            copy.wait()
        ready = here * rows // COLUMNS * COLUMNS
        for first in range(done, ready, COLUMNS):
            part = slice(first, first + COLUMNS)
            total = dot(dv, held[part], CONTRACT_LANES) + dot(g, down_ref[:, part], CONTRACT_ROWS)
            columns[:, part] = total.astype(BF16)
        part = pl.ds(done, ready - done)
        leaving.append(pltpu.make_async_copy(columns.at[:, part], out_ref.at[:, part], out_sem.at[group]))
        leaving[-1].start()
        done = ready
    for copy in leaving:
        copy.wait()


def snake(sizes):
    path = [0]
    for size in sizes:
        path = [i * size + k for at, i in enumerate(path) for k in (range(size) if at % 2 == 0 else reversed(range(size)))]
    return path


def exchange(value):
    return lax.all_to_all(value, "dp", split_axis=0, concat_axis=0, tiled=True)


def local(x, dv, weight, down, up, sequence_adapter, loss_length, owner_slot):
    devices = lax.axis_size("dp")
    tokens, width = x.shape
    value = dv.shape[1]
    rows = down.shape[0]
    chunk = value // devices
    ranks = devices * RANK
    slots = owner_slot.reshape(1, devices)

    chips = devices // 2
    side = int(chips ** 0.5)
    path = snake((chips // 4, 2, 2) if chips <= 16 else (side, chips // side))
    ring = [2 * chip + core for chip in path for core in range(2)]
    weights = lax.all_gather(weight, "dp", axis=0, tiled=True, axis_index_groups=[ring])

    own_up = up.reshape(RANK, devices, chunk).transpose(1, 0, 2)
    own_id = jnp.broadcast_to(sequence_adapter.astype(BF16).reshape(1, 1, 1), (devices, 1, LANES))
    packed = jnp.concatenate([own_up.reshape(devices, -1, LANES), own_id], axis=1)
    met = exchange(packed)
    met_up = met[:, :-1].reshape(devices, RANK, chunk)
    met_id = jnp.broadcast_to(met[:, -1:, :LANES - chunk], (devices, RANK, LANES - chunk))
    met = jnp.concatenate([met_up, met_id], axis=2).reshape(ranks, LANES)

    second = pl.pallas_call(
        functools.partial(pick_kernel, chunk),
        out_shape=jax.ShapeDtypeStruct((ranks, rows + chunk), BF16),
        in_specs=[VMEM, VMEM, VMEM],
        out_specs=VMEM,
        compiler_params=params(8),
    )(met, down, slots)
    got = exchange(second.reshape(devices, -1, LANES)).reshape(devices, RANK, rows + chunk)

    own_down, g, third = pl.pallas_call(
        functools.partial(rank_kernel, rows, chunk),
        out_shape=(
            jax.ShapeDtypeStruct((RANK, width), BF16),
            jax.ShapeDtypeStruct((RANK, tokens), BF16),
            jax.ShapeDtypeStruct((devices, RANK, rows + chunk), BF16),
        ),
        in_specs=[SMEM, VMEM, VMEM, VMEM],
        out_specs=(VMEM, VMEM, VMEM),
        scratch_shapes=[pltpu.VMEM((RANK, value), BF16)],
        compiler_params=params(8),
    )(loss_length, x, dv, got)
    sums = exchange(third.reshape(devices, -1, LANES)).reshape(ranks, rows + chunk)

    grad_down, slot_sums = pl.pallas_call(
        functools.partial(place_kernel, chunk),
        out_shape=(jax.ShapeDtypeStruct((rows, ranks), F32), jax.ShapeDtypeStruct((ranks, chunk), F32)),
        in_specs=[VMEM, VMEM, VMEM],
        out_specs=(VMEM, VMEM),
        compiler_params=params(8),
    )(met, slots, sums)
    fourth = exchange(slot_sums.reshape(devices, RANK, chunk))
    grad_up = fourth.transpose(1, 0, 2).reshape(RANK, value)

    order, block = path, 2 * rows
    if block % 16:
        back = sorted(range(chips), key=lambda position: path[position])
        weights = weights.reshape(chips, block, value)[jnp.array(back)].reshape(width, value)
    groups = 4
    if block % 16 or chips % groups:
        order, block = list(range(groups)), width // groups
    grad_x = pl.pallas_call(
        functools.partial(product_kernel, order),
        out_shape=jax.ShapeDtypeStruct((tokens, width), BF16),
        in_specs=[SMEM, VMEM, VMEM, VMEM, HBM],
        out_specs=HBM,
        scratch_shapes=[
            pltpu.VMEM((width, value), BF16),
            pltpu.VMEM((tokens, width), BF16),
            pltpu.SemaphoreType.DMA((len(order),)),
            pltpu.SemaphoreType.DMA((groups,)),
        ],
        compiler_params=params(60),
    )(loss_length, dv, g, own_down, weights)
    return grad_x, grad_down, grad_up


def solution(mesh):
    split = P(("groups", "dp"))
    rows = P(("groups", "dp"), None)
    shard = P("dp", None)
    return jax.shard_map(
        local,
        mesh=mesh,
        in_specs=(rows, rows, shard, shard, shard, split, split, P()),
        out_specs=(rows, rows, rows),
        check_vma=False,
    )
```

```python
import functools

import jax
import jax.numpy as jnp
from jax import lax
from jax.experimental import pallas as pl
from jax.experimental.pallas import tpu as pltpu
from jax.sharding import PartitionSpec as P

RANK = 16
LANES = 128
COLUMNS = 512
SCALE = 2.0
BF16 = jnp.bfloat16
F32 = jnp.float32
CONTRACT_LANES = (((1,), (1,)), ((), ()))
CONTRACT_ROWS = (((0,), (0,)), ((), ()))
CONTRACT_INNER = (((1,), (0,)), ((), ()))
VMEM = pl.BlockSpec(memory_space=pltpu.VMEM)
HBM = pl.BlockSpec(memory_space=pltpu.HBM)
SMEM = pl.BlockSpec(memory_space=pltpu.SMEM)


def dot(a, b, dims):
    return lax.dot_general(a, b, dims, preferred_element_type=F32)


def params(megabytes):
    return pltpu.CompilerParams(vmem_limit_bytes=megabytes << 20)


def selectors(met_ref, slots_ref, id_lane):
    rows = met_ref.shape[0]
    adapter = met_ref[:, id_lane:id_lane + 1].astype(F32).astype(jnp.int32)
    lane = lax.broadcasted_iota(jnp.int32, (rows, slots_ref.shape[1]), 1)
    slot = jnp.sum(jnp.where(lane == adapter, slots_ref[...], 0).astype(F32), axis=1, keepdims=True)
    slot = slot.astype(jnp.int32)
    column = lax.broadcasted_iota(jnp.int32, (rows, rows), 1)
    rank = lax.broadcasted_iota(jnp.int32, (rows, 1), 0) % RANK
    by_adapter = jnp.where(column == adapter * RANK + rank, 1.0, 0.0).astype(BF16)
    by_slot = jnp.where(column == slot * RANK + rank, 1.0, 0.0).astype(BF16)
    return by_adapter, by_slot


def pick_kernel(chunk, met_ref, down_ref, slots_ref, out_ref):
    by_adapter, by_slot = selectors(met_ref, slots_ref, chunk)
    rows = down_ref.shape[0]
    out_ref[:, :rows] = dot(by_adapter, down_ref[...], CONTRACT_LANES).astype(BF16)
    picked = dot(by_slot, met_ref[...], CONTRACT_INNER).astype(BF16)
    out_ref[:, rows:rows + chunk] = picked[:, :chunk]


def place_kernel(chunk, met_ref, slots_ref, sums_ref, down_ref, up_ref):
    by_adapter, by_slot = selectors(met_ref, slots_ref, chunk)
    rows = down_ref.shape[0]
    down_ref[...] = dot(sums_ref[:, :rows], by_adapter, CONTRACT_ROWS)
    up_ref[...] = dot(by_slot, sums_ref[:, rows:rows + chunk], CONTRACT_ROWS)


def masked(dv, length):
    position = lax.broadcasted_iota(jnp.int32, (dv.shape[0], 1), 0)
    return jnp.where(position < length, dv, jnp.zeros_like(dv))


def rank_kernel(rows, chunk, length_ref, x_ref, dv_ref, got_ref, down_ref, g_ref, out_ref, up_ref):
    devices = got_ref.shape[0]
    for j in range(devices):
        down_ref[:, j * rows:(j + 1) * rows] = got_ref[j, :, :rows]
        up_ref[:, j * chunk:(j + 1) * chunk] = got_ref[j, :, rows:rows + chunk]
    dv = masked(dv_ref[...], length_ref[0])
    g = (SCALE * dot(up_ref[...], dv, CONTRACT_LANES)).astype(BF16)
    g_ref[...] = g
    u = dot(down_ref[...], x_ref[...], CONTRACT_LANES).astype(BF16)
    down_sum = dot(g, x_ref[...], CONTRACT_INNER).astype(BF16)
    up_sum = (SCALE * dot(u, dv, CONTRACT_INNER)).astype(BF16)
    for j in range(devices):
        out_ref[j, :, :rows] = down_sum[:, j * rows:(j + 1) * rows]
        out_ref[j, :, rows:rows + chunk] = up_sum[:, j * chunk:(j + 1) * chunk]


def product_kernel(order, length_ref, dv_ref, g_ref, down_ref, w_ref, out_ref, *scratch):
    held, columns, adapter, sem, out_sem = scratch
    rows = held.shape[0] // len(order)
    copies = [None] * len(order)
    for position, block in enumerate(order):
        source = w_ref.at[pl.ds(position * rows, rows)]
        copies[block] = pltpu.make_async_copy(source, held.at[pl.ds(block * rows, rows)], sem.at[block])
    for copy in copies:
        copy.start()
    dv = masked(dv_ref[...], length_ref[0])
    g = g_ref[...]
    for first in range(0, held.shape[0], COLUMNS):
        part = slice(first, first + COLUMNS)
        adapter[:, part] = dot(g, down_ref[:, part], CONTRACT_ROWS)
    groups = out_sem.shape[0]
    leaving = []
    done = 0
    for group in range(groups):
        here = len(order) * (group + 1) // groups
        for copy in copies[len(order) * group // groups:here]:
            copy.wait()
        ready = here * rows // COLUMNS * COLUMNS
        for first in range(done, ready, COLUMNS):
            part = slice(first, first + COLUMNS)
            columns[:, part] = (dot(dv, held[part], CONTRACT_LANES) + adapter[:, part]).astype(BF16)
        part = pl.ds(done, ready - done)
        leaving.append(pltpu.make_async_copy(columns.at[:, part], out_ref.at[:, part], out_sem.at[group]))
        leaving[-1].start()
        done = ready
    for copy in leaving:
        copy.wait()


def snake(sizes):
    path = [0]
    for size in sizes:
        path = [i * size + k for at, i in enumerate(path) for k in (range(size) if at % 2 == 0 else reversed(range(size)))]
    return path


def exchange(value):
    return lax.all_to_all(value, "dp", split_axis=0, concat_axis=0, tiled=True)


def local(x, dv, weight, down, up, sequence_adapter, loss_length, owner_slot):
    devices = lax.axis_size("dp")
    tokens, width = x.shape
    value = dv.shape[1]
    rows = down.shape[0]
    chunk = value // devices
    ranks = devices * RANK
    slots = owner_slot.reshape(1, devices)

    chips = devices // 2
    side = int(chips ** 0.5)
    path = snake((chips // 4, 2, 2) if chips <= 16 else (side, chips // side))
    ring = [2 * chip + core for chip in path for core in range(2)]
    weights = lax.all_gather(weight, "dp", axis=0, tiled=True, axis_index_groups=[ring])

    own_up = up.reshape(RANK, devices, chunk).transpose(1, 0, 2)
    own_id = jnp.broadcast_to(sequence_adapter.astype(BF16).reshape(1, 1, 1), (devices, 1, LANES))
    packed = jnp.concatenate([own_up.reshape(devices, -1, LANES), own_id], axis=1)
    met = exchange(packed)
    met_up = met[:, :-1].reshape(devices, RANK, chunk)
    met_id = jnp.broadcast_to(met[:, -1:, :LANES - chunk], (devices, RANK, LANES - chunk))
    met = jnp.concatenate([met_up, met_id], axis=2).reshape(ranks, LANES)

    second = pl.pallas_call(
        functools.partial(pick_kernel, chunk),
        out_shape=jax.ShapeDtypeStruct((ranks, rows + chunk), BF16),
        in_specs=[VMEM, VMEM, VMEM],
        out_specs=VMEM,
        compiler_params=params(8),
    )(met, down, slots)
    got = exchange(second.reshape(devices, -1, LANES)).reshape(devices, RANK, rows + chunk)

    own_down, g, third = pl.pallas_call(
        functools.partial(rank_kernel, rows, chunk),
        out_shape=(
            jax.ShapeDtypeStruct((RANK, width), BF16),
            jax.ShapeDtypeStruct((RANK, tokens), BF16),
            jax.ShapeDtypeStruct((devices, RANK, rows + chunk), BF16),
        ),
        in_specs=[SMEM, VMEM, VMEM, VMEM],
        out_specs=(VMEM, VMEM, VMEM),
        scratch_shapes=[pltpu.VMEM((RANK, value), BF16)],
        compiler_params=params(8),
    )(loss_length, x, dv, got)
    sums = exchange(third.reshape(devices, -1, LANES)).reshape(ranks, rows + chunk)

    grad_down, slot_sums = pl.pallas_call(
        functools.partial(place_kernel, chunk),
        out_shape=(jax.ShapeDtypeStruct((rows, ranks), F32), jax.ShapeDtypeStruct((ranks, chunk), F32)),
        in_specs=[VMEM, VMEM, VMEM],
        out_specs=(VMEM, VMEM),
        compiler_params=params(8),
    )(met, slots, sums)
    fourth = exchange(slot_sums.reshape(devices, RANK, chunk))
    grad_up = fourth.transpose(1, 0, 2).reshape(RANK, value)

    order, block = path, 2 * rows
    if block % 16:
        back = sorted(range(chips), key=lambda position: path[position])
        weights = weights.reshape(chips, block, value)[jnp.array(back)].reshape(width, value)
    groups = 4
    if block % 16 or chips % groups:
        order, block = list(range(groups)), width // groups
    grad_x = pl.pallas_call(
        functools.partial(product_kernel, order),
        out_shape=jax.ShapeDtypeStruct((tokens, width), BF16),
        in_specs=[SMEM, VMEM, VMEM, VMEM, HBM],
        out_specs=HBM,
        scratch_shapes=[
            pltpu.VMEM((width, value), BF16),
            pltpu.VMEM((tokens, width), BF16),
            pltpu.VMEM((tokens, width), F32),
            pltpu.SemaphoreType.DMA((len(order),)),
            pltpu.SemaphoreType.DMA((groups,)),
        ],
        compiler_params=params(60),
    )(loss_length, dv, g, own_down, weights)
    return grad_x, grad_down, grad_up


def solution(mesh):
    split = P(("groups", "dp"))
    rows = P(("groups", "dp"), None)
    shard = P("dp", None)
    return jax.shard_map(
        local,
        mesh=mesh,
        in_specs=(rows, rows, shard, shard, shard, split, split, P()),
        out_specs=(rows, rows, rows),
        check_vma=False,
    )
```
